256 devices in a mesh: row: 32 (over z_hi, x, core), col: 8 (over z_lo, y).
Axes of the slice: x: 4, y: 4, z: 8 (z_hi: 4, z_lo: 2; z = z_hi * 2 + z_lo), core: 2. Of those that a mesh axis runs over, the one named last changes fastest.
Arguments:
- matrix: float32 [16384, 16384], P('row', 'col'), may hold values from -9 to 9
- reflectors: float32 [16384, 512], P('row'), may hold values from -0.046875 to 0.046875
- factor: float32 [512, 512], replicated, may hold values from -1 to 3, as said below
Outputs:
- updated: float32 [16384, 16384], P('row', 'col')
The draws below stay inside these ranges and needn't reach their ends.
Inputs may be any that keep to these rules, and one draw needn't show every extreme that they name: factor is upper triangular with diagonal entries of 1.5 to 2.5.
All inputs are finite; a program needn't handle non-finite values.
Results may differ from the reference program's by a relative error of at most 0.000064.
Values sent between devices are 32-bit elements; how exact they have to be, the bound alone decides.
A program may use at most 128 MiB of HBM per device.

```python
import jax
import jax.numpy as jnp
from jax import lax

N = 16384
K = 512


def draw_matrix(key, part):
    base = jnp.clip(jax.random.normal(key, (N, N), jnp.float32), -6.0, 6.0)
    return (base + base.T) * 0.70710678


def draw_factor(key, part):
    first_key, second_key = jax.random.split(jax.random.fold_in(key, 7))
    diagonal = jax.random.uniform(first_key, (K,), jnp.float32, 1.5, 2.5)
    upper = jnp.clip(jax.random.normal(second_key, (K, K), jnp.float32), -4.0, 4.0)
    upper = upper * K ** (-0.5)
    rows = jnp.arange(K)[:, None]
    columns = jnp.arange(K)[None, :]
    above = jnp.where(columns > rows, upper, 0.0)
    return above + jnp.where(columns == rows, diagonal[None, :], 0.0)


def block_levels(own_key, dims, cuts, smallest, largest):
    loudness = 1.0
    for position, shards_of in cuts:
        heights = jax.random.uniform(jax.random.fold_in(jax.random.fold_in(own_key, 6), position), (shards_of,), jnp.float32, smallest / len(cuts), largest / len(cuts))
        loudness = loudness * jnp.repeat(jnp.exp(heights), dims[position] // shards_of).reshape((-1,) + (1,) * (len(dims) - 1 - position))
    return loudness


def normal_values(key, extent, spread, reach, pieces=(), kind=jnp.bfloat16):
    level = block_levels(key, extent, pieces, -0.22, 0.18) if pieces else 1.0
    drawn = jax.random.normal(key, extent, jnp.float32) * spread * level
    return jnp.minimum(jnp.maximum(drawn, -reach), reach).astype(kind)


def setup_inputs(seed: int = 0) -> dict:
    splits = jax.random.split(jax.random.key(seed), 4)
    matrix = draw_matrix(jax.random.fold_in(splits[3], 71), 0)
    reflectors = normal_values(splits[1], (N, K), N ** -0.5, 0.046875, ((0, 32),), jnp.float32)
    factor = draw_factor(jax.random.fold_in(splits[3], 71), 0)
    return dict(matrix=matrix, reflectors=reflectors, factor=factor)


def precise_dot(left, right):
    return jnp.dot(left, right, preferred_element_type=jnp.float32, precision=lax.Precision.HIGHEST)


def reference(matrix, reflectors, factor):
    projected = precise_dot(matrix, reflectors)
    inner = precise_dot(reflectors.T, projected)
    middle = precise_dot(factor.T, precise_dot(inner, factor))
    w_full = precise_dot(projected, factor) - 0.5 * precise_dot(reflectors, middle)
    first = precise_dot(reflectors, w_full.T)
    second = precise_dot(w_full, reflectors.T)
    return matrix - first - second
```

```python
import functools

import jax
import jax.numpy as jnp
from jax import lax
from jax.experimental import pallas as pl
from jax.experimental.pallas import tpu as pltpu
from jax.sharding import PartitionSpec as P

MESH = pl.DeviceIdType.MESH
F32 = jnp.float32
BF16 = jnp.bfloat16
NN = (((1,), (0,)), ((), ()))
NT = (((1,), (1,)), ((), ()))


def split(value):
    high = value.astype(BF16)
    return high, (value - high.astype(F32)).astype(BF16)


def dot3(left, right, dims):
    dot = functools.partial(lax.dot_general, dimension_numbers=dims, preferred_element_type=F32)
    return dot(left[0], right[0]) + (dot(left[0], right[1]) + dot(left[1], right[0]))


def mod(value, size):
    return lax.rem(value + 4 * size, size)


def kernel(
    a_hbm, v_hbm, f_hbm, out,
    a, v, f, ah, al, vh, vl, gv, gvh, gvl, gz, gzh, gzl,
    gh, gl, yp, yrecv, zp, zr, zrh, zrl,
    inner, isib, ia, icol, ib, ix, ic, iz, full,
    local_sem, *sems,
):
    r, c = lax.axis_index("row"), lax.axis_index("col")
    zh, x, k = r // 8, lax.rem(r // 2, 4), lax.rem(r, 2)
    zl, y = c // 4, lax.rem(c, 4)

    def at(zh_, x_, k_, zl_, y_):
        return (zh_ * 8 + x_ * 2 + k_, zl_ * 4 + y_)

    sibling = at(zh, x, 1 - k, zl, y)

    def xdev(d):
        return at(zh, mod(x + d, 4), k, zl, y)

    def zdev(d):
        return at(mod(zh + d, 4), x, k, zl, y)

    def cdev(d):
        return at(zh, x, k, lax.rem(zl + d // 4, 2), mod(y + d, 4))

    zl_t = zh // 2
    y_t = lax.rem(zh, 2) * 2 + x // 2
    m_own = lax.rem(x, 2) * 2 + k

    def piece_of(zl_, y_):
        return zl_ * 256 + mod(zh + y_ - y_t + 2, 4) * 64

    own_piece = pl.multiple_of(piece_of(zl, y), 64)
    target = at(mod(zh + y - y_t + 2, 4), mod(2 * lax.rem(y_t, 2) + 3 * m_own, 4), zl, zl_t, y_t)
    target_row = pl.multiple_of(m_own * 512 + own_piece, 64)
    x0 = 2 * lax.rem(y, 2)
    m_here = lax.rem(3 * mod(x - x0, 4), 4)
    zh_s = 2 * zl + y // 2
    source = at(zh_s, 2 * lax.rem(y, 2) + m_here // 2, lax.rem(m_here, 2), k, mod(zh - zh_s - 2 + y, 4))

    def place(x_, z_):
        m = lax.rem(3 * mod(x_ - x0, 4), 4)
        return pl.multiple_of(m * 512 + k * 256 + mod(z_, 4) * 64, 64)

    loads = [
        pltpu.make_async_copy(v_hbm, v, local_sem.at[0]),
        pltpu.make_async_copy(f_hbm, f, local_sem.at[1]),
        pltpu.make_async_copy(a_hbm, a, local_sem.at[2]),
    ]
    for copy in loads:
        copy.start()

    barrier = pltpu.get_barrier_semaphore()
    greet = [sibling, source]
    greet += [xdev(d) for d in (1, 2, 3)] + [zdev(d) for d in (1, 2, 3)] + [cdev(d) for d in range(1, 8)]
    for device in greet:
        pl.semaphore_signal(barrier, inc=1, device_id=device, device_id_type=MESH)

    pending = []

    def send(src, dst, pair, index, device):
        copy = pltpu.make_async_remote_copy(
            src_ref=src, dst_ref=dst,
            send_sem=pair[0].at[index], recv_sem=pair[1].at[index],
            device_id=device, device_id_type=MESH,
        )
        copy.start()
        pending.append(copy)
        return copy

    it = iter(range(0, len(sems), 2))

    def pair():
        i = next(it)
        return sems[i], sems[i + 1]

    class Gather:
        def __init__(self, buf):
            self.buf = buf
            self.scatter_sem, self.z_sem, self.x_sem, self.f_sem, self.s_sem = [pair() for _ in range(5)]

        def rows(self, start, count=64):
            return self.buf.at[pl.ds(start, count)]

        def scatter(self, src):
            self.first = send(src, self.rows(target_row), self.scatter_sem, 0, target)

        def spread(self, o):
            here = place(x, zh - o)
            for i, d in enumerate((1, -1)):
                self.x[o, d] = send(self.rows(here), self.rows(here), self.x_sem, o * 2 + i, xdev(d))
            self.s[o, 0] = send(self.rows(here), self.rows(here), self.s_sem, o * 4, sibling)

        def begin(self):
            self.x, self.z, self.s, self.f = {}, {}, {}, {}
            self.first.wait_recv()
            here = place(x, zh)
            for d in (2, 1, 3):
                self.z[d] = send(self.rows(here), self.rows(here), self.z_sem, d - 1, zdev(d))
            self.spread(0)

        def zstep(self, o):
            self.z[o].wait_recv()
            self.spread(o)

        def xstep(self, o):
            for i, d in enumerate((1, -1)):
                self.x[o, d].wait_recv()
                here = place(x - d, zh - o)
                half = pl.multiple_of(here + 32 * i, 32)
                self.f[o, d] = send(self.rows(half, 32), self.rows(half, 32), self.f_sem, o * 2 + i, xdev(d))
                self.s[o, d] = send(self.rows(here), self.rows(here), self.s_sem, o * 4 + 1 + i, sibling)

        def fstep(self, o):
            for d in (1, -1):
                self.f[o, d].wait_recv()
            here = place(x + 2, zh - o)
            self.s[o, 2] = send(self.rows(here), self.rows(here), self.s_sem, o * 4 + 3, sibling)

        def end(self, o):
            for j in (0, 1, -1, 2):
                self.s[o, j].wait_recv()

    gather_v, gather_z = Gather(gv), Gather(gz)
    y_sem, ag_sem, is_sem, ic_sem, ix_sem, iz_sem, ex_sem, ec_sem, es_sem = [pair() for _ in range(9)]

    loads[0].wait()
    pl.semaphore_wait(barrier, len(greet))
    gather_v.scatter(v.at[pl.ds(own_piece, 64)])

    def split_into(src, high, low, rows, step):
        @pl.loop(0, rows // step)
        def _(i):
            at_ = pl.ds(pl.multiple_of(i * step, step), step)
            high[at_], low[at_] = split(src[at_])

    loads[1].wait()
    split_into(v, vh, vl, 512, 64)
    gh[...], gl[...] = split(dot3((vh[...], vl[...]), split(f[...]), NT))
    loads[2].wait()
    split_into(a, ah, al, 512, 16)

    gather_v.begin()
    gather_v.zstep(1)
    gather_v.zstep(3)
    gather_v.xstep(0)
    gather_v.zstep(2)
    gather_v.xstep(1)
    gather_v.xstep(3)
    gather_v.fstep(0)
    gather_v.fstep(1)
    gather_v.fstep(3)
    gather_v.xstep(2)
    gather_v.fstep(2)
    for o in (0, 1, 3, 2):
        gather_v.end(o)
    split_into(gv, gvh, gvl, 2048, 64)

    @pl.loop(0, 2)
    def _(i):
        at_ = pl.ds(pl.multiple_of(i * 256, 256), 256)
        yp[at_] = dot3((ah[at_], al[at_]), (gvh[...], gvl[...]), NN)

    sums = []
    for d in (6, 2, 5, 7, 1, 3, 4):
        row = pl.multiple_of(piece_of(lax.rem(zl + d // 4, 2), mod(y + d, 4)), 64)
        sums.append(send(yp.at[pl.ds(row, 64)], yrecv.at[d - 1], y_sem, d - 1, cdev(d)))

    part = dot3(
        (vh[...].T, vl[...].T), split(yp[...]), NN
    )
    inner[...] = 0.5 * (part + part.T)
    other = pl.ds(pl.multiple_of((1 - k) * 256, 256), 256)
    s1 = send(inner.at[other], isib, is_sem, 0, sibling)

    for copy in sums:
        copy.wait_recv()
    total = yp[pl.ds(own_piece, 64)]
    for d in range(7):
        total += yrecv[d]
    zp[...] = dot3(split(total), split(f[...]), NN)
    gather_z.scatter(zp)
    zr[pl.ds(own_piece, 64)] = zp[...]
    ag = []
    for d in (6, 2, 5, 7, 1, 3, 4):
        ag.append(send(zp, zr.at[pl.ds(own_piece, 64)], ag_sem, d - 1, cdev(d)))

    s1.wait_recv()
    ia[...] = inner[pl.ds(pl.multiple_of(k * 256, 256), 256)] + isib[...]
    s2 = []
    for d in (6, 2, 5, 7, 1, 3, 4):
        row = pl.multiple_of((lax.rem(zl + d // 4, 2) * 4 + mod(y + d, 4)) * 32, 32)
        s2.append(send(ia.at[pl.ds(row, 32)], icol.at[d - 1], ic_sem, d - 1, cdev(d)))

    gather_z.begin()

    for copy in s2:
        copy.wait_recv()
    total = ia[pl.ds(pl.multiple_of(c * 32, 32), 32)]
    for d in range(7):
        total += icol[d]
    ib[...] = total
    s3 = []
    for d in (2, 1, 3):
        row = pl.multiple_of(mod(x + d, 4) * 8, 8)
        s3.append(send(ib.at[pl.ds(row, 8)], ix.at[d - 1], ix_sem, d - 1, xdev(d)))

    gather_z.zstep(1)
    gather_z.zstep(3)
    gather_z.xstep(0)

    for copy in s3:
        copy.wait_recv()
    total = ib[pl.ds(pl.multiple_of(x * 8, 8), 8)]
    for d in range(3):
        total += ix[d]
    ic[...] = total
    s4 = [send(ic, iz.at[d - 1], iz_sem, d - 1, zdev(d)) for d in (2, 1, 3)]

    gather_z.zstep(2)
    gather_z.xstep(1)

    for copy in s4:
        copy.wait_recv()
    total = ic[...]
    for d in range(3):
        total += iz[d]
    mine = pl.ds(pl.multiple_of(k * 256 + c * 32 + x * 8, 8), 8)
    full[mine] = dot3(split(total), split(f[...]), NN)
    s5 = [send(full.at[mine], full.at[mine], ex_sem, d - 1, xdev(d)) for d in (2, 1, 3)]

    gather_z.xstep(3)
    gather_z.fstep(0)

    for copy in s5:
        copy.wait_recv()
    mine = pl.ds(pl.multiple_of(k * 256 + c * 32, 32), 32)
    s6 = [send(full.at[mine], full.at[mine], ec_sem, d - 1, cdev(d)) for d in (6, 2, 5, 7, 1, 3, 4)]

    gather_z.fstep(1)
    gather_z.fstep(3)
    gather_z.xstep(2)

    for copy in s6:
        copy.wait_recv()
    mine = pl.ds(pl.multiple_of(k * 256, 256), 256)
    s7 = send(full.at[mine], full.at[mine], es_sem, 0, sibling)
    gather_z.fstep(2)
    s7.wait_recv()
    for copy in ag:
        copy.wait_recv()
    zrh[...], zrl[...] = split(zr[...] - dot3((gh[...], gl[...]), split(full[...]), NN))

    for o in (0, 1, 3, 2):
        gather_z.end(o)
    split_into(gz, gzh, gzl, 2048, 64)

    @pl.loop(0, 8)
    def _(i):
        at_ = pl.ds(pl.multiple_of(i * 256, 256), 256)
        first = dot3((vh[...], vl[...]), (gzh[at_], gzl[at_]), NT)
        second = dot3((zrh[...], zrl[...]), (gvh[at_], gvl[at_]), NT)
        out[:, at_] = first + second

    for copy in pending:
        copy.wait_send()


def local(matrix, reflectors, factor):
    vmem = pltpu.VMEM
    dma = pltpu.SemaphoreType.DMA
    gather_sems = [1, 3, 8, 8, 16]
    pairs = gather_sems * 2 + [7, 7, 1, 7, 3, 3, 3, 7, 1]
    sems = []
    for count in pairs:
        sems += [dma((count,)), dma((count,))]
    block, panel, tall = (512, 2048), (512, 512), (2048, 512)
    update = pl.pallas_call(
        kernel,
        out_shape=jax.ShapeDtypeStruct(block, F32),
        in_specs=[pl.BlockSpec(memory_space=pl.ANY)] * 3,
        out_specs=pl.BlockSpec(memory_space=pltpu.VMEM),
        scratch_shapes=[
            vmem(block, F32), vmem(panel, F32), vmem(panel, F32), vmem(block, BF16), vmem(block, BF16),
            vmem(panel, BF16), vmem(panel, BF16),
            vmem(tall, F32), vmem(tall, BF16), vmem(tall, BF16), vmem(tall, F32), vmem(tall, BF16), vmem(tall, BF16),
            vmem(panel, BF16), vmem(panel, BF16), vmem(panel, F32), vmem((7, 64, 512), F32), vmem((64, 512), F32),
            vmem(panel, F32), vmem(panel, BF16), vmem(panel, BF16),
            vmem(panel, F32), vmem((256, 512), F32), vmem((256, 512), F32), vmem((7, 32, 512), F32),
            vmem((32, 512), F32), vmem((3, 8, 512), F32), vmem((8, 512), F32), vmem((3, 8, 512), F32), vmem(panel, F32),
            dma((3,)), *sems,
        ],
        compiler_params=pltpu.CompilerParams(collective_id=0, has_side_effects=True, vmem_limit_bytes=56 << 20),
        name="panel_update",
    )(matrix, reflectors, factor)
    return matrix - update


def solution(mesh):
    placed = (P("row", "col"), P("row", None), P())
    return jax.shard_map(
        local, mesh=mesh, in_specs=placed, out_specs=P("row", "col"), check_vma=False
    )
```

```python
import functools

import jax
import jax.numpy as jnp
from jax import lax
from jax.experimental import pallas as pl
from jax.experimental.pallas import tpu as pltpu
from jax.sharding import PartitionSpec as P

MESH = pl.DeviceIdType.MESH
F32 = jnp.float32
BF16 = jnp.bfloat16
NN = (((1,), (0,)), ((), ()))
NT = (((1,), (1,)), ((), ()))


def split(value):
    high = value.astype(BF16)
    return high, (value - high.astype(F32)).astype(BF16)


def dot3(left, right, dims):
    (axis,), (other,) = dims[0]
    return lax.dot_general(
        jnp.concatenate([left[0], left[1], left[0]], axis),
        jnp.concatenate([right[0], right[0], right[1]], other),
        dims,
        preferred_element_type=F32,
    )


def mod(value, size):
    return lax.rem(value + 4 * size, size)


CHUNKS = 4


def kernel(
    a_hbm, v_hbm, f_hbm, out_hbm, out,
    a, v, f, ah, al, vh, vl, fh, fl, gv, gvh, gvl, gz, gzh, gzl,
    gh, gl, yp, yrecv, yown, yother, yfin, yth, ytl, zp, zr, zrh, zrl,
    part, inner, isib, ia, icol, ib, ix, ic, iz, full,
    local_sem, out_sem, *sems,
):
    nq = CHUNKS
    kc = 512 // nq
    r, c = lax.axis_index("row"), lax.axis_index("col")
    zh, x, k = r // 8, lax.rem(r // 2, 4), lax.rem(r, 2)
    zl, y = c // 4, lax.rem(c, 4)

    def at(zh_, x_, k_, zl_, y_):
        return (zh_ * 8 + x_ * 2 + k_, zl_ * 4 + y_)

    sibling = at(zh, x, 1 - k, zl, y)
    partner = at(zh, x, k, 1 - zl, y)

    def xdev(d):
        return at(zh, mod(x + d, 4), k, zl, y)

    def zdev(d):
        return at(mod(zh + d, 4), x, k, zl, y)

    def ydev(d):
        return at(zh, x, k, zl, mod(y + d, 4))

    def cdev(d):
        return at(zh, x, k, lax.rem(zl + d // 4, 2), mod(y + d, 4))

    zl_t = zh // 2
    y_t = lax.rem(zh, 2) * 2 + x // 2
    m_own = lax.rem(x, 2) * 2 + k
    x_t = mod(2 * lax.rem(y_t, 2) + 3 * m_own, 4)
    k_t = mod(zl + k + 1 + zl_t, 2)
    o_own = mod(y - y_t, 4)

    def piece_of(zl_, y_):
        return pl.multiple_of(mod(zl_ + k + 1 + zl_t, 2) * 256 + mod(y_ - y_t, 4) * 64, 64)

    own_piece = piece_of(zl, y)
    target_row = pl.multiple_of(m_own * 512 + own_piece, 64)

    def target(d):
        return at(mod(zh + d, 4), x_t, k_t, zl_t, y_t)

    x0 = 2 * lax.rem(y, 2)
    m_here = lax.rem(3 * mod(x - x0, 4), 4)
    k_s = lax.rem(m_here, 2)
    zl_s = mod(k + k_s + 1 + zl, 2)

    def source(o):
        return at(2 * zl + y // 2, x0 + m_here // 2, k_s, zl_s, mod(y + o, 4))

    def place(x_, o):
        m = lax.rem(3 * mod(x_ - x0, 4), 4)
        return pl.multiple_of(m * 512 + k * 256 + o * 64, 64)

    loads = [
        pltpu.make_async_copy(v_hbm, v, local_sem.at[0]),
        pltpu.make_async_copy(f_hbm, f, local_sem.at[1]),
        pltpu.make_async_copy(a_hbm, a, local_sem.at[2]),
    ]
    for copy in loads:
        copy.start()

    barrier = pltpu.get_barrier_semaphore()
    greet = [source(o) for o in range(4)] + [sibling]
    greet += [xdev(d) for d in (1, 2, 3)] + [zdev(d) for d in (1, 2, 3)] + [cdev(d) for d in range(1, 8)]
    for device in greet:
        pl.semaphore_signal(barrier, inc=1, device_id=device, device_id_type=MESH)

    it = iter(sems)

    def copy_of(src, dst, send_sem, recv_sem, device):
        return pltpu.make_async_remote_copy(
            src_ref=src, dst_ref=dst, send_sem=send_sem, recv_sem=recv_sem, device_id=device, device_id_type=MESH
        )

    class Moves:
        def __init__(self):
            self.sent, self.came = next(it), next(it)

        def send(self, group, src, dst, device):
            copy_of(src, dst, self.sent.at[0], self.came.at[group], device).start()

        def wait(self, group, like):
            copy_of(like, like, self.sent.at[0], self.came.at[group], sibling).wait_recv()

        def drain(self, like):
            copy_of(like, like, self.sent.at[0], self.came.at[0], sibling).wait_send()

    class Gather:
        def __init__(self, buf):
            self.buf, self.moves = buf, Moves()

        def rows(self, start, count):
            return self.buf.at[pl.ds(start, count)]

        def scatter(self, src):
            for d in (0, 1, 3, 2):
                self.moves.send(o_own // 2, src, self.rows(target_row, 64), target(d))

        def p(self, g):
            self.moves.wait(g, self.rows(0, 128))
            here = self.rows(place(x, 2 * g), 128)
            for d in (1, 3):
                self.moves.send(2 + g, here, here, xdev(d))
            self.moves.send(4, here, here, sibling)

        def x(self, g):
            self.moves.wait(2 + g, self.rows(0, 256))
            for d, o in ((1, 2 * g), (3, 2 * g + 1)):
                half = self.rows(place(x - d, o), 64)
                self.moves.send(5 + g, half, half, xdev(d))
            for d in (1, 3):
                here = self.rows(place(x - d, 2 * g), 128)
                self.moves.send(4, here, here, sibling)

        def f(self, g):
            self.moves.wait(5 + g, self.rows(0, 128))
            here = self.rows(place(x + 2, 2 * g), 128)
            self.moves.send(4, here, here, sibling)

        def end(self):
            self.moves.wait(4, self.rows(0, 1024))

        def drain(self):
            self.moves.drain(self.buf)

    gather_v = [Gather(gv.at[q]) for q in range(nq)]
    gather_z = [Gather(gz.at[q]) for q in range(nq)]
    rs = [Moves() for q in range(nq)]
    ag = [Moves() for q in range(nq)]
    red = [Moves() for _ in range(7)]

    def split_into(src, high, low, rows, step, columns=slice(None)):
        @pl.loop(0, rows // step)
        def _(i):
            at_ = pl.ds(pl.multiple_of(i * step, step), step)
            high[at_, columns], low[at_, columns] = split(src[at_])

    def cols(q):
        return pl.ds(q * kc, kc)

    keep = {}

    def v_scatter(q):
        gather_v[q].scatter(v.at[pl.ds(own_piece, 64), cols(q)])

    def y_block(q):
        gather_v[q].end()
        split_into(gv.at[q], gvh, gvl, 2048, 64, cols(q))
        right = jnp.concatenate([gvh[:, cols(q)], gvl[:, cols(q)]], 1)

        @pl.loop(0, 2)
        def _(i):
            at_ = pl.ds(pl.multiple_of(i * 256, 256), 256)
            both = jnp.dot(ah[at_], right, preferred_element_type=F32)
            yp[q, at_] = both[:, :kc] + (both[:, kc:] + jnp.dot(al[at_], right[:, :kc], preferred_element_type=F32))

        for d in (2, 1, 3):
            for e in (0, 1):
                row = piece_of(lax.rem(zl + e, 2), mod(y + d, 4))
                rs[q].send(0, yp.at[q, pl.ds(row, 64)], yrecv.at[q, d - 1, e], ydev(d))

    def rs_mid(q):
        rs[q].wait(0, yp.at[q, pl.ds(0, 384)])
        for e, dst in enumerate((yown, yother)):
            total = yp[q, pl.ds(piece_of(lax.rem(zl + e, 2), y), 64)]
            for d in range(3):
                total += yrecv[q, d, e]
            dst[q] = total
        rs[q].send(1, yother.at[q], yfin.at[q], partner)

    def z_block(q):
        rs[q].wait(1, yfin.at[q])
        yth[q], ytl[q] = split(yown[q] + yfin[q])
        total = 0
        for p in range(q + 1):
            total += dot3((yth[p], ytl[p]), (fh[p * kc : p * kc + kc, cols(q)], fl[p * kc : p * kc + kc, cols(q)]), NN)
        zp[q] = total
        gather_z[q].scatter(zp.at[q])
        zr[q, pl.ds(own_piece, 64)] = total

    def ag_start(q):
        mine = zr.at[q, pl.ds(own_piece, 64)]
        ag[q].send(0, zp.at[q], mine, partner)
        for d in (2, 1, 3):
            ag[q].send(1, zp.at[q], mine, ydev(d))

    def ag_mid(q):
        ag[q].wait(0, zp.at[q])
        theirs = zr.at[q, pl.ds(piece_of(1 - zl, y), 64)]
        for d in (2, 1, 3):
            ag[q].send(1, theirs, theirs, ydev(d))

    def i_start():
        vt = (vh[...].T, vl[...].T)
        part[...] = dot3(vt, split(jnp.concatenate([yp[q] for q in range(nq)], 1)), NN)
        inner[...] = 0.5 * (part[...] + part[...].T)
        other = pl.ds(pl.multiple_of((1 - k) * 256, 256), 256)
        red[0].send(0, inner.at[other], isib, sibling)

    def i_col():
        red[0].wait(0, isib)
        ia[...] = inner[pl.ds(pl.multiple_of(k * 256, 256), 256)] + isib[...]
        for d in (6, 2, 5, 7, 1, 3, 4):
            row = pl.multiple_of((lax.rem(zl + d // 4, 2) * 4 + mod(y + d, 4)) * 32, 32)
            red[1].send(0, ia.at[pl.ds(row, 32)], icol.at[d - 1], cdev(d))

    def i_x():
        red[1].wait(0, icol)
        total = ia[pl.ds(pl.multiple_of(c * 32, 32), 32)]
        for d in range(7):
            total += icol[d]
        ib[...] = total
        for d in (2, 1, 3):
            row = pl.multiple_of(mod(x + d, 4) * 8, 8)
            red[2].send(0, ib.at[pl.ds(row, 8)], ix.at[d - 1], xdev(d))

    def i_z():
        red[2].wait(0, ix)
        total = ib[pl.ds(pl.multiple_of(x * 8, 8), 8)]
        for d in range(3):
            total += ix[d]
        ic[...] = total
        for d in (2, 1, 3):
            red[3].send(0, ic, iz.at[d - 1], zdev(d))

    def i_f():
        red[3].wait(0, iz)
        total = ic[...]
        for d in range(3):
            total += iz[d]
        mine = pl.ds(pl.multiple_of(k * 256 + c * 32 + x * 8, 8), 8)
        full[mine] = dot3(split(total), (fh[...], fl[...]), NN)
        for d in (2, 1, 3):
            red[4].send(0, full.at[mine], full.at[mine], xdev(d))

    def i_ag():
        red[4].wait(0, ix)
        mine = pl.ds(pl.multiple_of(k * 256 + c * 32, 32), 32)
        for d in (6, 2, 5, 7, 1, 3, 4):
            red[5].send(0, full.at[mine], full.at[mine], cdev(d))

    def i_sib():
        red[5].wait(0, icol)
        mine = pl.ds(pl.multiple_of(k * 256, 256), 256)
        red[6].send(0, full.at[mine], full.at[mine], sibling)

    def second():
        red[6].wait(0, isib)
        right = split(full[...])
        rows = dot3((gh[...], gl[...]), right, NN)
        for q in range(nq):
            ag[q].wait(1, yp.at[q, pl.ds(0, 384)])
            zrh[:, cols(q)], zrl[:, cols(q)] = split(zr[q] - rows[:, q * kc : q * kc + kc])
        product(lambda at_: dot3((zrh[...], zrl[...]), (gvh[at_], gvl[at_]), NT), last=True)

    def product(value, last=False):
        fresh = "out" not in keep
        keep["out"] = True

        @pl.loop(0, 8)
        def _(i):
            at_ = pl.ds(pl.multiple_of(i * 256, 256), 256)
            if fresh:
                out[:, at_] = value(at_)
            else:
                out[:, at_] += value(at_)
            if last:
                pltpu.make_async_copy(out.at[:, at_], out_hbm.at[:, at_], out_sem.at[i]).start()

        if last:
            for i in range(8):
                at_ = pl.ds(i * 256, 256)
                pltpu.make_async_copy(out.at[:, at_], out_hbm.at[:, at_], out_sem.at[i]).wait()

    def first(p):
        pair_ = pl.ds(p * 256, 256)
        for q in range(p * nq // 2, (p + 1) * nq // 2):
            gather_z[q].end()
            split_into(gz.at[q], gzh, gzl, 2048, 64, cols(q))
        product(lambda at_: dot3((vh[:, pair_], vl[:, pair_]), (gzh[at_, pair_], gzl[at_, pair_]), NT))

    steps = dict(vs=v_scatter, y=y_block, rm=rs_mid, z=z_block, as_=ag_start, am=ag_mid, fst=first)

    def run(name):
        if name in single:
            single[name]()
        elif name[:-1] in steps:
            steps[name[:-1]](int(name[-1]))
        else:
            which, q, part_, g = name
            gather = (gather_v if which == "v" else gather_z)[int(q)]
            dict(p=gather.p, x=gather.x, f=gather.f)[part_](int(g))

    loads[0].wait()
    split_into(v, vh, vl, 512, 64)
    loads[1].wait()
    fh[...], fl[...] = split(f[...])
    pl.semaphore_wait(barrier, len(greet))

    def local_work():
        loads[2].wait()
        split_into(a, ah, al, 512, 16)
        gh[...], gl[...] = split(dot3((vh[...], vl[...]), (fh[...], fl[...]), NT))

    single = dict(
        local=local_work, i0=i_start, i1=i_col, i2=i_x, i3=i_z, i4=i_f, i5=i_ag, i6=i_sib, sec=second
    )
    for name in PROGRAM:
        run(name)
    for gather in gather_v + gather_z:
        gather.drain()
    for q in range(nq):
        rs[q].drain(yp.at[q, pl.ds(0, 448)])
        ag[q].drain(yp.at[q, pl.ds(0, 448)])
    for moves, like in zip(red, (isib, icol, ix, iz, ix, icol, isib), strict=True):
        moves.drain(like)


PROGRAM = (
    "vs0", "local", "vs1", "vs2", "vs3", "v0p0", "v0p1", "v1p0", "v1p1", "v0x0", "v2p0", "v0x1", "v2p1", "v1x0",
    "v3p0", "v1x1", "v0f0", "v3p1", "v2x0", "v0f1", "v2x1", "v1f0", "y0", "v3x0", "v1f1", "v3x1", "v2f0", "y1",
    "v3f0", "v2f1", "v3f1", "rm0", "y2", "y3", "rm1", "z0", "i0", "z1", "rm2", "i1", "rm3", "z2", "z0p0", "z0p1",
    "z1p0", "z1p1", "z0x0", "z3", "i2", "as_2", "as_0", "as_3", "z0x1", "as_1", "z1x0", "z1x1", "z0f0", "z2p0",
    "i3", "z0f1", "z2p1", "am2", "z1f0", "am0", "z1f1", "z3p0", "am3", "am1", "z2x0", "z3p1", "fst0", "i4",
    "z3x0", "z2x1", "z2f0", "z3x1", "i5", "z3f0", "z2f1", "z3f1", "fst1", "i6", "sec"
)


def local(matrix, reflectors, factor):
    vmem = pltpu.VMEM
    dma = pltpu.SemaphoreType.DMA
    nq = CHUNKS
    kc = 512 // nq
    sems = []
    for groups in [7] * (2 * nq) + [2] * (2 * nq) + [1] * 7:
        sems += [dma((1,)), dma((groups,))]
    block, panel, tall, wide = (512, 2048), (512, 512), (nq, 2048, kc), (nq, 512, kc)
    piece, flat = (nq, 64, kc), (2048, 512)
    update = pl.pallas_call(
        kernel,
        out_shape=jax.ShapeDtypeStruct(block, F32),
        in_specs=[pl.BlockSpec(memory_space=pl.ANY)] * 3,
        out_specs=pl.BlockSpec(memory_space=pl.ANY),
        scratch_shapes=[
            vmem(block, F32), vmem(block, F32), vmem(panel, F32), vmem(panel, F32), vmem(block, BF16), vmem(block, BF16),
            vmem(panel, BF16), vmem(panel, BF16), vmem(panel, BF16), vmem(panel, BF16),
            vmem(tall, F32), vmem(flat, BF16), vmem(flat, BF16), vmem(tall, F32), vmem(flat, BF16), vmem(flat, BF16),
            vmem(panel, BF16), vmem(panel, BF16), vmem(wide, F32), vmem((nq, 3, 2, 64, kc), F32),
            vmem(piece, F32), vmem(piece, F32), vmem(piece, F32), vmem(piece, BF16), vmem(piece, BF16), vmem(piece, F32),
            vmem(wide, F32), vmem(panel, BF16), vmem(panel, BF16),
            vmem(panel, F32), vmem(panel, F32), vmem((256, 512), F32), vmem((256, 512), F32), vmem((7, 32, 512), F32),
            vmem((32, 512), F32), vmem((3, 8, 512), F32), vmem((8, 512), F32), vmem((3, 8, 512), F32), vmem(panel, F32),
            dma((3,)), dma((8,)), *sems,
        ],
        compiler_params=pltpu.CompilerParams(collective_id=0, has_side_effects=True, vmem_limit_bytes=56 << 20),
        name="panel_update",
    )(matrix, reflectors, factor)
    return matrix - update


def solution(mesh):
    placed = (P("row", "col"), P("row", None), P())
    return jax.shard_map(
        local, mesh=mesh, in_specs=placed, out_specs=P("row", "col"), check_vma=False
    )
```

```python
import functools

import jax
import jax.numpy as jnp
from jax import lax
from jax.experimental import pallas as pl
from jax.experimental.pallas import tpu as pltpu
from jax.sharding import PartitionSpec as P

MESH = pl.DeviceIdType.MESH
F32 = jnp.float32
BF16 = jnp.bfloat16
NN = (((1,), (0,)), ((), ()))
NT = (((1,), (1,)), ((), ()))


def split(value):
    high = value.astype(BF16)
    return high, (value - high.astype(F32)).astype(BF16)


def dot3(left, right, dims):
    (axis,), (other,) = dims[0]
    return lax.dot_general(
        jnp.concatenate([left[0], left[1], left[0]], axis),
        jnp.concatenate([right[0], right[0], right[1]], other),
        dims,
        preferred_element_type=F32,
    )


def mod(value, size):
    return lax.rem(value + 4 * size, size)


CHUNKS = 4


def kernel(
    a_hbm, v_hbm, f_hbm, base_hbm, zh_hbm, zl_hbm, base,
    a, v, f, ah, al, vh, vl, fh, fl, gv, gvh, gvl, gz, gzh, gzl,
    gh, gl, yp, yrecv, yown, yother, yfin, yth, ytl, zp, zr, zrh, zrl,
    vth, vtl, local_sem, out_sem, *rest,
):
    nq = CHUNKS
    kc = 512 // nq
    r, c = lax.axis_index("row"), lax.axis_index("col")
    zh, x, k = r // 8, lax.rem(r // 2, 4), lax.rem(r, 2)
    zl, y = c // 4, lax.rem(c, 4)

    def at(zh_, x_, k_, zl_, y_):
        return (zh_ * 8 + x_ * 2 + k_, zl_ * 4 + y_)

    sibling = at(zh, x, 1 - k, zl, y)
    partner = at(zh, x, k, 1 - zl, y)

    def xdev(d):
        return at(zh, mod(x + d, 4), k, zl, y)

    def zdev(d):
        return at(mod(zh + d, 4), x, k, zl, y)

    def ydev(d):
        return at(zh, x, k, zl, mod(y + d, 4))

    def cdev(d):
        return at(zh, x, k, lax.rem(zl + d // 4, 2), mod(y + d, 4))

    zl_t = zh // 2
    y_t = lax.rem(zh, 2) * 2 + x // 2
    m_own = lax.rem(x, 2) * 2 + k
    x_t = mod(2 * lax.rem(y_t, 2) + 3 * m_own, 4)
    k_t = mod(zl + k + 1 + zl_t, 2)
    o_own = mod(y - y_t, 4)

    def piece_of(zl_, y_):
        return pl.multiple_of(mod(zl_ + k + 1 + zl_t, 2) * 256 + mod(y_ - y_t, 4) * 64, 64)

    own_piece = piece_of(zl, y)
    target_row = pl.multiple_of(m_own * 512 + own_piece, 64)

    def target(d):
        return at(mod(zh + d, 4), x_t, k_t, zl_t, y_t)

    x0 = 2 * lax.rem(y, 2)
    m_here = lax.rem(3 * mod(x - x0, 4), 4)
    k_s = lax.rem(m_here, 2)
    zl_s = mod(k + k_s + 1 + zl, 2)

    def source(o):
        return at(2 * zl + y // 2, x0 + m_here // 2, k_s, zl_s, mod(y + o, 4))

    def place(x_, o):
        m = lax.rem(3 * mod(x_ - x0, 4), 4)
        return pl.multiple_of(m * 512 + k * 256 + o * 64, 64)

    loads = [
        pltpu.make_async_copy(v_hbm, v, local_sem.at[0]),
        pltpu.make_async_copy(f_hbm, f, local_sem.at[1]),
        pltpu.make_async_copy(a_hbm, a, local_sem.at[2]),
    ]
    for copy in loads:
        copy.start()

    barrier = pltpu.get_barrier_semaphore()
    greet = [source(o) for o in range(4)] + [sibling]
    greet += [xdev(d) for d in (1, 2, 3)] + [zdev(d) for d in (1, 2, 3)] + [cdev(d) for d in range(1, 8)]
    for device in greet:
        pl.semaphore_signal(barrier, inc=1, device_id=device, device_id_type=MESH)

    sums, sems = rest[:18], rest[18:]
    it = iter(sems)

    def copy_of(src, dst, send_sem, recv_sem, device):
        return pltpu.make_async_remote_copy(
            src_ref=src, dst_ref=dst, send_sem=send_sem, recv_sem=recv_sem, device_id=device, device_id_type=MESH
        )

    class Moves:
        def __init__(self):
            self.sent, self.came = next(it), next(it)

        def send(self, group, src, dst, device):
            copy_of(src, dst, self.sent.at[0], self.came.at[group], device).start()

        def wait(self, group, like):
            copy_of(like, like, self.sent.at[0], self.came.at[group], sibling).wait_recv()

        def drain(self, like):
            copy_of(like, like, self.sent.at[0], self.came.at[0], sibling).wait_send()

    class Gather:
        def __init__(self, buf):
            self.buf, self.moves = buf, Moves()

        def rows(self, start, count):
            return self.buf.at[pl.ds(start, count)]

        def scatter(self, src):
            for d in (0, 1, 3, 2):
                self.moves.send(o_own // 2, src, self.rows(target_row, 64), target(d))

        def p(self, g):
            self.moves.wait(g, self.rows(0, 128))
            here = self.rows(place(x, 2 * g), 128)
            for d in (1, 3):
                self.moves.send(2 + g, here, here, xdev(d))
            self.moves.send(4, here, here, sibling)

        def x(self, g):
            self.moves.wait(2 + g, self.rows(0, 256))
            for d, o in ((1, 2 * g), (3, 2 * g + 1)):
                half = self.rows(place(x - d, o), 64)
                self.moves.send(5 + g, half, half, xdev(d))
            for d in (1, 3):
                here = self.rows(place(x - d, 2 * g), 128)
                self.moves.send(4, here, here, sibling)

        def f(self, g):
            self.moves.wait(5 + g, self.rows(0, 128))
            here = self.rows(place(x + 2, 2 * g), 128)
            self.moves.send(4, here, here, sibling)

        def end(self):
            self.moves.wait(4, self.rows(0, 1024))

        def drain(self):
            self.moves.drain(self.buf)

    gather_v = [Gather(gv.at[q]) for q in range(nq)]
    gather_z = [Gather(gz.at[q]) for q in range(nq)]
    rs = [Moves() for q in range(nq)]
    ag = [Moves() for q in range(nq)]
    red = {tag: [Moves() for _ in range(7)] for tag in "ab"}
    held = dict(a=sums[:9], b=sums[9:])

    def split_into(src, high, low, rows, step, columns=slice(None)):
        @pl.loop(0, rows // step)
        def _(i):
            at_ = pl.ds(pl.multiple_of(i * step, step), step)
            high[at_, columns], low[at_, columns] = split(src[at_])

    def cols(q):
        return pl.ds(q * kc, kc)

    keep = {}

    def v_scatter(q):
        gather_v[q].scatter(v.at[pl.ds(own_piece, 64), cols(q)])

    def y_block(q):
        gather_v[q].end()
        split_into(gv.at[q], gvh, gvl, 2048, 64, cols(q))
        right = jnp.concatenate([gvh[:, cols(q)], gvl[:, cols(q)]], 1)

        @pl.loop(0, 2)
        def _(i):
            at_ = pl.ds(pl.multiple_of(i * 256, 256), 256)
            both = jnp.dot(ah[at_], right, preferred_element_type=F32)
            yp[q, at_] = both[:, :kc] + (both[:, kc:] + jnp.dot(al[at_], right[:, :kc], preferred_element_type=F32))

        for d in (2, 1, 3):
            for e in (0, 1):
                row = piece_of(lax.rem(zl + e, 2), mod(y + d, 4))
                rs[q].send(0, yp.at[q, pl.ds(row, 64)], yrecv.at[q, d - 1, e], ydev(d))

    def rs_mid(q):
        rs[q].wait(0, yp.at[q, pl.ds(0, 384)])
        for e, dst in enumerate((yown, yother)):
            total = yp[q, pl.ds(piece_of(lax.rem(zl + e, 2), y), 64)]
            for d in range(3):
                total += yrecv[q, d, e]
            dst[q] = total
        rs[q].send(1, yother.at[q], yfin.at[q], partner)

    def z_block(q):
        rs[q].wait(1, yfin.at[q])
        yth[q], ytl[q] = split(yown[q] + yfin[q])
        total = 0
        for p in range(q + 1):
            total += dot3((yth[p], ytl[p]), (fh[p * kc : p * kc + kc, cols(q)], fl[p * kc : p * kc + kc, cols(q)]), NN)
        zp[q] = total
        gather_z[q].scatter(zp.at[q])
        zr[q, pl.ds(own_piece, 64)] = total

    def ag_start(q):
        mine = zr.at[q, pl.ds(own_piece, 64)]
        ag[q].send(0, zp.at[q], mine, partner)
        for d in (2, 1, 3):
            ag[q].send(1, zp.at[q], mine, ydev(d))

    def ag_mid(q):
        ag[q].wait(0, zp.at[q])
        theirs = zr.at[q, pl.ds(piece_of(1 - zl, y), 64)]
        for d in (2, 1, 3):
            ag[q].send(1, theirs, theirs, ydev(d))

    def i_start(tag):
        part = held[tag][0]
        if tag == "a":
            vth[...], vtl[...] = vh[...].T, vl[...].T
            right = split(jnp.concatenate([yp[q] for q in range(nq // 2)], 1))
            part[...] = dot3((vth[...], vtl[...]), right, NN)
        else:
            right = split(jnp.concatenate([yp[q] for q in range(nq // 2, nq)], 1))
            block = dot3((vth[256:], vtl[256:]), right, NN)
            part[0:256], part[256:512] = block[:, :128], block[:, 128:]
        other = pl.ds(pl.multiple_of((1 - k) * 256, 256), 256)
        red[tag][0].send(0, part.at[other], held[tag][1], sibling)

    def i_col(tag):
        part, isib, ia, icol = held[tag][:4]
        red[tag][0].wait(0, isib)
        ia[...] = part[pl.ds(pl.multiple_of(k * 256, 256), 256)] + isib[...]
        for d in (6, 2, 5, 7, 1, 3, 4):
            row = pl.multiple_of((lax.rem(zl + d // 4, 2) * 4 + mod(y + d, 4)) * 32, 32)
            red[tag][1].send(0, ia.at[pl.ds(row, 32)], icol.at[d - 1], cdev(d))

    def i_x(tag):
        ia, icol, ib, ix = held[tag][2:6]
        red[tag][1].wait(0, icol)
        total = ia[pl.ds(pl.multiple_of(c * 32, 32), 32)]
        for d in range(7):
            total += icol[d]
        ib[...] = total
        for d in (2, 1, 3):
            row = pl.multiple_of(mod(x + d, 4) * 8, 8)
            red[tag][2].send(0, ib.at[pl.ds(row, 8)], ix.at[d - 1], xdev(d))

    def i_z(tag):
        ib, ix, ic, iz = held[tag][4:8]
        red[tag][2].wait(0, ix)
        total = ib[pl.ds(pl.multiple_of(x * 8, 8), 8)]
        for d in range(3):
            total += ix[d]
        ic[...] = total
        for d in (2, 1, 3):
            red[tag][3].send(0, ic, iz.at[d - 1], zdev(d))

    def i_f(tag):
        ic, iz, full = held[tag][6:]
        red[tag][3].wait(0, iz)
        total = ic[...]
        for d in range(3):
            total += iz[d]
        mine = pl.ds(pl.multiple_of(k * 256 + c * 32 + x * 8, 8), 8)
        full[mine] = total
        for d in (2, 1, 3):
            red[tag][4].send(0, full.at[mine], full.at[mine], xdev(d))

    def i_ag(tag):
        full = held[tag][8]
        red[tag][4].wait(0, held[tag][5])
        mine = pl.ds(pl.multiple_of(k * 256 + c * 32, 32), 32)
        for d in (6, 2, 5, 7, 1, 3, 4):
            red[tag][5].send(0, full.at[mine], full.at[mine], cdev(d))

    def i_sib(tag):
        full = held[tag][8]
        red[tag][5].wait(0, held[tag][3])
        mine = pl.ds(pl.multiple_of(k * 256, 256), 256)
        red[tag][6].send(0, full.at[mine], full.at[mine], sibling)

    def second():
        for tag in "ab":
            red[tag][6].wait(0, held[tag][1])
        left, corner = held["a"][8][...], held["b"][8]
        low = jnp.concatenate([corner[0:256], corner[256:512]], 1)
        inner = jnp.concatenate([left, jnp.concatenate([left[256:].T, low], 0)], 1)
        rows = dot3(split(dot3((gh[...], gl[...]), split(inner), NN)), (fh[...], fl[...]), NN)
        for q in range(nq):
            ag[q].wait(1, yp.at[q, pl.ds(0, 384)])
            zrh[:, cols(q)], zrl[:, cols(q)] = split(zr[q] - rows[:, q * kc : q * kc + kc])

    def blocks(start, count, body):
        @pl.loop(start, start + count)
        def _(i):
            body(i, pl.ds(pl.multiple_of(i * 256, 256), 256))

    def second_part(p):
        def body(i, at_):
            base[:, at_] = a[:, at_] - dot3((zrh[...], zrl[...]), (gvh[at_], gvl[at_]), NT)
            pltpu.make_async_copy(base.at[:, at_], base_hbm.at[:, at_], out_sem.at[i]).start()

        blocks(2 * p, 2, body)

    def z_out(q):
        return [
            pltpu.make_async_copy(src.at[:, cols(q)], dst.at[:, cols(q)], out_sem.at[8 + 2 * q + i])
            for i, (src, dst) in enumerate(((gzh, zh_hbm), (gzl, zl_hbm)))
        ]

    def z_split(q):
        gather_z[q].end()
        split_into(gz.at[q], gzh, gzl, 2048, 64, cols(q))
        for copy in z_out(q):
            copy.start()

    def finish():
        for i in range(8):
            at_ = pl.ds(i * 256, 256)
            pltpu.make_async_copy(base.at[:, at_], base_hbm.at[:, at_], out_sem.at[i]).wait()
        for q in range(nq):
            for copy in z_out(q):
                copy.wait()

    reduce_steps = (i_start, i_col, i_x, i_z, i_f, i_ag, i_sib)
    steps = dict(vs=v_scatter, y=y_block, rm=rs_mid, z=z_block, as_=ag_start, am=ag_mid, zs=z_split, sp=second_part)

    def run(name):
        if name in single:
            single[name]()
        elif name[0] == "i":
            reduce_steps[int(name[1])](name[2])
        elif name[:-1] in steps:
            steps[name[:-1]](int(name[-1]))
        else:
            which, q, part_, g = name
            gather = (gather_v if which == "v" else gather_z)[int(q)]
            dict(p=gather.p, x=gather.x, f=gather.f)[part_](int(g))

    loads[0].wait()
    split_into(v, vh, vl, 512, 64)
    loads[1].wait()
    fh[...], fl[...] = split(f[...])
    pl.semaphore_wait(barrier, len(greet))

    def local_work():
        loads[2].wait()
        split_into(a, ah, al, 512, 16)
        gh[...], gl[...] = split(dot3((vh[...], vl[...]), (fh[...], fl[...]), NT))

    single = dict(local=local_work, tr=second, end=finish)
    for name in PROGRAM:
        run(name)
    for gather in gather_v + gather_z:
        gather.drain()
    for q in range(nq):
        rs[q].drain(yp.at[q, pl.ds(0, 448)])
        ag[q].drain(yp.at[q, pl.ds(0, 448)])
    for tag in "ab":
        _, isib, _, icol, _, ix, _, iz, _ = held[tag]
        for moves, like in zip(red[tag], (isib, icol, ix, iz, ix, icol, isib), strict=True):
            moves.drain(like)


PROGRAM = (
    "vs0", "vs1", "local", "vs2", "vs3", "v0p0", "v0p1", "v1p0", "v1p1", "v0x0", "v2p0", "v0x1", "v2p1", "v1x0",
    "v3p0", "v1x1", "v0f0", "v3p1", "v2x0", "v0f1", "v2x1", "v1f0", "y0", "v3x0", "v1f1", "v3x1", "v2f0", "v2f1",
    "y1", "v3f0", "i0a", "y2", "v3f1", "rm0", "i1a", "y3", "z0", "i0b", "rm1", "rm2", "i1b", "i2a", "z1", "z2",
    "rm3", "i3a", "i2b", "as_0", "as_1", "as_2", "z0p0", "z0p1", "i3b", "z1p0", "z0x0", "z1p1", "z3", "as_3",
    "i4a", "z0x1", "z2p0", "am0", "am1", "z2p1", "am2", "i4b", "z1x0", "z0f0", "z1x1", "z0f1", "am3", "i5a",
    "z2x0", "z3p0", "z3p1", "zs0", "z2x1", "z1f0", "i5b", "z1f1", "z2f0", "z3x0", "i6a", "z3x1", "zs1", "z2f1",
    "i6b", "z3f0", "tr", "zs2", "z3f1", "sp0", "sp1", "zs3", "sp2", "sp3", "end"
)


def last_kernel(v_hbm, base_hbm, zh_hbm, zl_hbm, out_hbm, v, base, zh, zl, vh, vl, in_sem, out_sem):
    def block(i):
        return pl.ds(pl.multiple_of(i * 256, 256), 256)

    def arrivals(i):
        at_ = block(i)
        return (
            pltpu.make_async_copy(zh_hbm.at[at_], zh.at[at_], in_sem.at[0, i]),
            pltpu.make_async_copy(zl_hbm.at[at_], zl.at[at_], in_sem.at[1, i]),
            pltpu.make_async_copy(base_hbm.at[:, at_], base.at[:, at_], in_sem.at[2, i]),
        )

    def leaving(i):
        at_ = block(i)
        return pltpu.make_async_copy(base.at[:, at_], out_hbm.at[:, at_], out_sem.at[i])

    own = pltpu.make_async_copy(v_hbm, v, out_sem.at[8])
    own.start()
    for i in range(8):
        for copy in arrivals(i):
            copy.start()
    own.wait()
    vh[...], vl[...] = split(v[...])

    @pl.loop(0, 8)
    def _(i):
        at_ = block(i)
        for copy in arrivals(i):
            copy.wait()
        base[:, at_] = base[:, at_] - dot3((vh[...], vl[...]), (zh[at_], zl[at_]), NT)
        leaving(i).start()

    for i in range(8):
        leaving(i).wait()


def local(matrix, reflectors, factor):
    vmem = pltpu.VMEM
    dma = pltpu.SemaphoreType.DMA
    nq = CHUNKS
    kc = 512 // nq
    sums = []
    for width in (256, 128):
        for rows in ((512,), (256,), (256,), (7, 32), (32,), (3, 8), (8,), (3, 8), (512,)):
            sums.append(vmem((*rows, width), F32))
    sems = []
    for groups in [7] * (2 * nq) + [2] * (2 * nq) + [1] * 14:
        sems += [dma((1,)), dma((groups,))]
    block, panel, tall, wide = (512, 2048), (512, 512), (nq, 2048, kc), (nq, 512, kc)
    piece, flat = (nq, 64, kc), (2048, 512)
    base, z_high, z_low = pl.pallas_call(
        kernel,
        out_shape=[
            jax.ShapeDtypeStruct(block, F32), jax.ShapeDtypeStruct(flat, BF16), jax.ShapeDtypeStruct(flat, BF16)
        ],
        in_specs=[pl.BlockSpec(memory_space=pl.ANY)] * 3,
        out_specs=[pl.BlockSpec(memory_space=pl.ANY)] * 3,
        scratch_shapes=[
            vmem(block, F32), vmem(block, F32), vmem(panel, F32), vmem(panel, F32), vmem(block, BF16), vmem(block, BF16),
            vmem(panel, BF16), vmem(panel, BF16), vmem(panel, BF16), vmem(panel, BF16),
            vmem(tall, F32), vmem(flat, BF16), vmem(flat, BF16), vmem(tall, F32), vmem(flat, BF16), vmem(flat, BF16),
            vmem(panel, BF16), vmem(panel, BF16), vmem(wide, F32), vmem((nq, 3, 2, 64, kc), F32),
            vmem(piece, F32), vmem(piece, F32), vmem(piece, F32), vmem(piece, BF16), vmem(piece, BF16), vmem(piece, F32),
            vmem(wide, F32), vmem(panel, BF16), vmem(panel, BF16),
            vmem(panel, BF16), vmem(panel, BF16), dma((3,)), dma((8 + 2 * nq,)), *sums, *sems,
        ],
        compiler_params=pltpu.CompilerParams(collective_id=0, has_side_effects=True, vmem_limit_bytes=56 << 20),
        name="panel_update",
    )(matrix, reflectors, factor)
    return pl.pallas_call(
        last_kernel,
        out_shape=jax.ShapeDtypeStruct(block, F32),
        in_specs=[pl.BlockSpec(memory_space=pl.ANY)] * 4,
        out_specs=pl.BlockSpec(memory_space=pl.ANY),
        scratch_shapes=[
            vmem(panel, F32), vmem(block, F32), vmem(flat, BF16), vmem(flat, BF16), vmem(panel, BF16), vmem(panel, BF16),
            dma((3, 8)), dma((9,)),
        ],
        compiler_params=pltpu.CompilerParams(vmem_limit_bytes=60 << 20),
        name="last_product",
    )(reflectors, base, z_high, z_low)


def solution(mesh):
    placed = (P("row", "col"), P("row", None), P())
    return jax.shard_map(
        local, mesh=mesh, in_specs=placed, out_specs=P("row", "col"), check_vma=False
    )
```

```python
import functools

import jax
import jax.numpy as jnp
from jax import lax
from jax.experimental import pallas as pl
from jax.experimental.pallas import tpu as pltpu
from jax.sharding import PartitionSpec as P

MESH = pl.DeviceIdType.MESH
F32 = jnp.float32
BF16 = jnp.bfloat16
NN = (((1,), (0,)), ((), ()))
NT = (((1,), (1,)), ((), ()))


def split(value):
    high = value.astype(BF16)
    return high, (value - high.astype(F32)).astype(BF16)


def dot3(left, right, dims):
    (axis,), (other,) = dims[0]
    return lax.dot_general(
        jnp.concatenate([left[0], left[1], left[0]], axis),
        jnp.concatenate([right[0], right[0], right[1]], other),
        dims,
        preferred_element_type=F32,
    )


def mod(value, size):
    return lax.rem(value + 4 * size, size)


CHUNKS = 4


def kernel(
    a_hbm, v_hbm, f_hbm, base_hbm, zh_hbm, zl_hbm, base,
    a, v, f, ah, al, vh, vl, fh, fl, gv, gvh, gvl, gz, gzh, gzl,
    gh, gl, yp, yrecv, yown, yother, yfin, yth, ytl, zp, zr, zrh, zrl,
    vth, vtl, local_sem, out_sem, *rest,
):
    nq = CHUNKS
    kc = 512 // nq
    r, c = lax.axis_index("row"), lax.axis_index("col")
    zh, x, k = r // 8, lax.rem(r // 2, 4), lax.rem(r, 2)
    zl, y = c // 4, lax.rem(c, 4)

    def at(zh_, x_, k_, zl_, y_):
        return (zh_ * 8 + x_ * 2 + k_, zl_ * 4 + y_)

    sibling = at(zh, x, 1 - k, zl, y)
    partner = at(zh, x, k, 1 - zl, y)

    def xdev(d):
        return at(zh, mod(x + d, 4), k, zl, y)

    def zdev(d):
        return at(mod(zh + d, 4), x, k, zl, y)

    def ydev(d):
        return at(zh, x, k, zl, mod(y + d, 4))

    def cdev(d):
        return at(zh, x, k, lax.rem(zl + d // 4, 2), mod(y + d, 4))

    zl_t = zh // 2
    y_t = lax.rem(zh, 2) * 2 + x // 2
    m_own = lax.rem(x, 2) * 2 + k
    x_t = mod(2 * lax.rem(y_t, 2) + 3 * m_own, 4)
    k_t = mod(zl + k + 1 + zl_t, 2)
    o_own = mod(y - y_t, 4)

    def piece_of(zl_, y_):
        return pl.multiple_of(mod(zl_ + k + 1 + zl_t, 2) * 256 + mod(y_ - y_t, 4) * 64, 64)

    own_piece = piece_of(zl, y)
    target_row = pl.multiple_of(m_own * 512 + own_piece, 64)

    def target(d):
        return at(mod(zh + d, 4), x_t, k_t, zl_t, y_t)

    x0 = 2 * lax.rem(y, 2)
    m_here = lax.rem(3 * mod(x - x0, 4), 4)
    k_s = lax.rem(m_here, 2)
    zl_s = mod(k + k_s + 1 + zl, 2)

    def source(o):
        return at(2 * zl + y // 2, x0 + m_here // 2, k_s, zl_s, mod(y + o, 4))

    def place(x_, o):
        m = lax.rem(3 * mod(x_ - x0, 4), 4)
        return pl.multiple_of(m * 512 + k * 256 + o * 64, 64)

    loads = [
        pltpu.make_async_copy(v_hbm, v, local_sem.at[0]),
        pltpu.make_async_copy(f_hbm, f, local_sem.at[1]),
        pltpu.make_async_copy(a_hbm, a, local_sem.at[2]),
    ]
    for copy in loads:
        copy.start()

    barrier = pltpu.get_barrier_semaphore()
    greet = [source(o) for o in range(4)] + [sibling]
    greet += [xdev(d) for d in (1, 2, 3)] + [zdev(d) for d in (1, 2, 3)] + [cdev(d) for d in range(1, 8)]
    for device in greet:
        pl.semaphore_signal(barrier, inc=1, device_id=device, device_id_type=MESH)

    sums, sems = rest[:18], rest[18:]
    it = iter(sems)

    def copy_of(src, dst, send_sem, recv_sem, device):
        return pltpu.make_async_remote_copy(
            src_ref=src, dst_ref=dst, send_sem=send_sem, recv_sem=recv_sem, device_id=device, device_id_type=MESH
        )

    class Moves:
        def __init__(self):
            self.sent, self.came = next(it), next(it)

        def send(self, group, src, dst, device):
            copy_of(src, dst, self.sent.at[0], self.came.at[group], device).start()

        def wait(self, group, like):
            copy_of(like, like, self.sent.at[0], self.came.at[group], sibling).wait_recv()

        def drain(self, like):
            copy_of(like, like, self.sent.at[0], self.came.at[0], sibling).wait_send()

    class Gather:
        def __init__(self, buf):
            self.buf, self.moves = buf, Moves()

        def rows(self, start, count):
            return self.buf.at[pl.ds(start, count)]

        def scatter(self, src):
            for d in (0, 1, 3, 2):
                self.moves.send(o_own // 2, src, self.rows(target_row, 64), target(d))

        def p(self, g):
            self.moves.wait(g, self.rows(0, 128))
            here = self.rows(place(x, 2 * g), 128)
            for d in (1, 3):
                self.moves.send(2 + g, here, here, xdev(d))
            self.moves.send(4, here, here, sibling)

        def x(self, g):
            self.moves.wait(2 + g, self.rows(0, 256))
            for d, o in ((1, 2 * g), (3, 2 * g + 1)):
                half = self.rows(place(x - d, o), 64)
                self.moves.send(5 + g, half, half, xdev(d))
            for d in (1, 3):
                here = self.rows(place(x - d, 2 * g), 128)
                self.moves.send(4, here, here, sibling)

        def f(self, g):
            self.moves.wait(5 + g, self.rows(0, 128))
            here = self.rows(place(x + 2, 2 * g), 128)
            self.moves.send(4, here, here, sibling)

        def end(self):
            self.moves.wait(4, self.rows(0, 1024))

        def drain(self):
            self.moves.drain(self.buf)

    gather_v = [Gather(gv.at[q]) for q in range(nq)]
    gather_z = [Gather(gz.at[q]) for q in range(nq)]
    rs = [Moves() for q in range(nq)]
    ag = [Moves() for q in range(nq)]
    red = {tag: [Moves() for _ in range(7)] for tag in "ab"}
    held = dict(a=sums[:9], b=sums[9:])

    def split_into(src, high, low, rows, step, columns=slice(None)):
        @pl.loop(0, rows // step)
        def _(i):
            at_ = pl.ds(pl.multiple_of(i * step, step), step)
            high[at_, columns], low[at_, columns] = split(src[at_])

    def cols(q):
        return pl.ds(q * kc, kc)

    keep = {}

    def v_scatter(q):
        gather_v[q].scatter(v_hbm.at[pl.ds(own_piece, 64), cols(q)])

    def y_block(q):
        gather_v[q].end()
        split_into(gv.at[q], gvh, gvl, 2048, 64, cols(q))
        right = jnp.concatenate([gvh[:, cols(q)], gvl[:, cols(q)]], 1)

        @pl.loop(0, 2)
        def _(i):
            at_ = pl.ds(pl.multiple_of(i * 256, 256), 256)
            both = jnp.dot(ah[at_], right, preferred_element_type=F32)
            yp[q, at_] = both[:, :kc] + (both[:, kc:] + jnp.dot(al[at_], right[:, :kc], preferred_element_type=F32))

        for d in (2, 1, 3):
            for e in (0, 1):
                row = piece_of(lax.rem(zl + e, 2), mod(y + d, 4))
                rs[q].send(0, yp.at[q, pl.ds(row, 64)], yrecv.at[q, d - 1, e], ydev(d))

    def rs_mid(q):
        rs[q].wait(0, yp.at[q, pl.ds(0, 384)])
        for e, dst in enumerate((yown, yother)):
            total = yp[q, pl.ds(piece_of(lax.rem(zl + e, 2), y), 64)]
            for d in range(3):
                total += yrecv[q, d, e]
            dst[q] = total
        rs[q].send(1, yother.at[q], yfin.at[q], partner)

    def z_block(q):
        rs[q].wait(1, yfin.at[q])
        yth[q], ytl[q] = split(yown[q] + yfin[q])
        total = 0
        for p in range(q + 1):
            total += dot3((yth[p], ytl[p]), (fh[p * kc : p * kc + kc, cols(q)], fl[p * kc : p * kc + kc, cols(q)]), NN)
        zp[q] = total
        gather_z[q].scatter(zp.at[q])
        zr[q, pl.ds(own_piece, 64)] = total

    def ag_start(q):
        mine = zr.at[q, pl.ds(own_piece, 64)]
        ag[q].send(0, zp.at[q], mine, partner)
        for d in (2, 1, 3):
            ag[q].send(1, zp.at[q], mine, ydev(d))

    def ag_mid(q):
        ag[q].wait(0, zp.at[q])
        theirs = zr.at[q, pl.ds(piece_of(1 - zl, y), 64)]
        for d in (2, 1, 3):
            ag[q].send(1, theirs, theirs, ydev(d))

    def i_start(tag):
        part = held[tag][0]
        if tag == "a":
            vth[...], vtl[...] = vh[...].T, vl[...].T
            right = split(jnp.concatenate([yp[q] for q in range(nq // 2)], 1))
            part[...] = dot3((vth[...], vtl[...]), right, NN)
        else:
            right = split(jnp.concatenate([yp[q] for q in range(nq // 2, nq)], 1))
            block = dot3((vth[256:], vtl[256:]), right, NN)
            part[0:256], part[256:512] = block[:, :128], block[:, 128:]
        other = pl.ds(pl.multiple_of((1 - k) * 256, 256), 256)
        red[tag][0].send(0, part.at[other], held[tag][1], sibling)

    def i_col(tag):
        part, isib, ia, icol = held[tag][:4]
        red[tag][0].wait(0, isib)
        ia[...] = part[pl.ds(pl.multiple_of(k * 256, 256), 256)] + isib[...]
        for d in (6, 2, 5, 7, 1, 3, 4):
            row = pl.multiple_of((lax.rem(zl + d // 4, 2) * 4 + mod(y + d, 4)) * 32, 32)
            red[tag][1].send(0, ia.at[pl.ds(row, 32)], icol.at[d - 1], cdev(d))

    def i_x(tag):
        ia, icol, ib, ix = held[tag][2:6]
        red[tag][1].wait(0, icol)
        total = ia[pl.ds(pl.multiple_of(c * 32, 32), 32)]
        for d in range(7):
            total += icol[d]
        ib[...] = total
        for d in (2, 1, 3):
            row = pl.multiple_of(mod(x + d, 4) * 8, 8)
            red[tag][2].send(0, ib.at[pl.ds(row, 8)], ix.at[d - 1], xdev(d))

    def i_z(tag):
        ib, ix, ic, iz = held[tag][4:8]
        red[tag][2].wait(0, ix)
        total = ib[pl.ds(pl.multiple_of(x * 8, 8), 8)]
        for d in range(3):
            total += ix[d]
        ic[...] = total
        for d in (2, 1, 3):
            red[tag][3].send(0, ic, iz.at[d - 1], zdev(d))

    def i_f(tag):
        ic, iz, full = held[tag][6:]
        red[tag][3].wait(0, iz)
        total = ic[...]
        for d in range(3):
            total += iz[d]
        mine = pl.ds(pl.multiple_of(k * 256 + c * 32 + x * 8, 8), 8)
        full[mine] = total
        for d in (2, 1, 3):
            red[tag][4].send(0, full.at[mine], full.at[mine], xdev(d))

    def i_ag(tag):
        full = held[tag][8]
        red[tag][4].wait(0, held[tag][5])
        mine = pl.ds(pl.multiple_of(k * 256 + c * 32, 32), 32)
        for d in (6, 2, 5, 7, 1, 3, 4):
            red[tag][5].send(0, full.at[mine], full.at[mine], cdev(d))

    def i_sib(tag):
        full = held[tag][8]
        red[tag][5].wait(0, held[tag][3])
        mine = pl.ds(pl.multiple_of(k * 256, 256), 256)
        red[tag][6].send(0, full.at[mine], full.at[mine], sibling)

    def second():
        for tag in "ab":
            red[tag][6].wait(0, held[tag][1])
        left, corner = held["a"][8][...], held["b"][8]
        low = jnp.concatenate([corner[0:256], corner[256:512]], 1)
        inner = jnp.concatenate([left, jnp.concatenate([left[256:].T, low], 0)], 1)
        rows = dot3(split(dot3((gh[...], gl[...]), split(inner), NN)), (fh[...], fl[...]), NN)
        for q in range(nq):
            ag[q].wait(1, yp.at[q, pl.ds(0, 384)])
            zrh[:, cols(q)], zrl[:, cols(q)] = split(zr[q] - rows[:, q * kc : q * kc + kc])

    def blocks(start, count, body):
        @pl.loop(start, start + count)
        def _(i):
            body(i, pl.ds(pl.multiple_of(i * 256, 256), 256))

    def second_part(p):
        def body(i, at_):
            base[:, at_] = a[:, at_] - dot3((zrh[...], zrl[...]), (gvh[at_], gvl[at_]), NT)
            pltpu.make_async_copy(base.at[:, at_], base_hbm.at[:, at_], out_sem.at[i]).start()

        blocks(2 * p, 2, body)

    def z_out(q):
        return [
            pltpu.make_async_copy(src.at[:, cols(q)], dst.at[:, cols(q)], out_sem.at[8 + 2 * q + i])
            for i, (src, dst) in enumerate(((gzh, zh_hbm), (gzl, zl_hbm)))
        ]

    def z_split(q):
        gather_z[q].end()
        split_into(gz.at[q], gzh, gzl, 2048, 64, cols(q))
        for copy in z_out(q):
            copy.start()

    def finish():
        for i in range(8):
            at_ = pl.ds(i * 256, 256)
            pltpu.make_async_copy(base.at[:, at_], base_hbm.at[:, at_], out_sem.at[i]).wait()
        for q in range(nq):
            for copy in z_out(q):
                copy.wait()

    reduce_steps = (i_start, i_col, i_x, i_z, i_f, i_ag, i_sib)
    steps = dict(vs=v_scatter, y=y_block, rm=rs_mid, z=z_block, as_=ag_start, am=ag_mid, zs=z_split, sp=second_part)

    def run(name):
        if name in single:
            single[name]()
        elif name[0] == "i":
            reduce_steps[int(name[1])](name[2])
        elif name[:-1] in steps:
            steps[name[:-1]](int(name[-1]))
        else:
            which, q, part_, g = name
            gather = (gather_v if which == "v" else gather_z)[int(q)]
            dict(p=gather.p, x=gather.x, f=gather.f)[part_](int(g))

    pl.semaphore_wait(barrier, len(greet))

    def local_work():
        loads[0].wait()
        split_into(v, vh, vl, 512, 64)
        loads[1].wait()
        fh[...], fl[...] = split(f[...])
        loads[2].wait()
        split_into(a, ah, al, 512, 16)
        gh[...], gl[...] = split(dot3((vh[...], vl[...]), (fh[...], fl[...]), NT))

    single = dict(local=local_work, tr=second, end=finish)
    for name in PROGRAM:
        run(name)
    for gather in gather_v + gather_z:
        gather.drain()
    for q in range(nq):
        rs[q].drain(yp.at[q, pl.ds(0, 448)])
        ag[q].drain(yp.at[q, pl.ds(0, 448)])
    for tag in "ab":
        _, isib, _, icol, _, ix, _, iz, _ = held[tag]
        for moves, like in zip(red[tag], (isib, icol, ix, iz, ix, icol, isib), strict=True):
            moves.drain(like)


PROGRAM = (
    "vs0", "vs1", "local", "vs2", "vs3", "v0p0", "v0p1", "v1p0", "v1p1", "v0x0", "v2p0", "v0x1", "v2p1", "v1x0",
    "v3p0", "v1x1", "v0f0", "v3p1", "v2x0", "v0f1", "v2x1", "v1f0", "y0", "v3x0", "v1f1", "v3x1", "v2f0", "v2f1",
    "y1", "v3f0", "i0a", "y2", "v3f1", "rm0", "i1a", "y3", "z0", "i0b", "rm1", "rm2", "i1b", "i2a", "z1", "z2",
    "rm3", "i3a", "i2b", "as_0", "as_1", "as_2", "z0p0", "z0p1", "i3b", "z1p0", "z0x0", "z1p1", "z3", "as_3",
    "i4a", "z0x1", "z2p0", "am0", "am1", "z2p1", "am2", "i4b", "z1x0", "z0f0", "z1x1", "z0f1", "am3", "i5a",
    "z2x0", "z3p0", "z3p1", "zs0", "z2x1", "z1f0", "i5b", "z1f1", "z2f0", "z3x0", "i6a", "z3x1", "zs1", "z2f1",
    "i6b", "z3f0", "tr", "zs2", "z3f1", "sp0", "sp1", "zs3", "sp2", "sp3", "end"
)


def last_kernel(v_hbm, base_hbm, zh_hbm, zl_hbm, out_hbm, v, base, zh, zl, vh, vl, in_sem, out_sem):
    def block(i):
        return pl.ds(pl.multiple_of(i * 256, 256), 256)

    def arrivals(i):
        at_ = block(i)
        return (
            pltpu.make_async_copy(zh_hbm.at[at_], zh.at[at_], in_sem.at[0, i]),
            pltpu.make_async_copy(zl_hbm.at[at_], zl.at[at_], in_sem.at[1, i]),
            pltpu.make_async_copy(base_hbm.at[:, at_], base.at[:, at_], in_sem.at[2, i]),
        )

    def leaving(i):
        at_ = block(i)
        return pltpu.make_async_copy(base.at[:, at_], out_hbm.at[:, at_], out_sem.at[i])

    own = pltpu.make_async_copy(v_hbm, v, out_sem.at[8])
    own.start()
    for i in range(8):
        for copy in arrivals(i):
            copy.start()
    own.wait()
    vh[...], vl[...] = split(v[...])

    @pl.loop(0, 8)
    def _(i):
        at_ = block(i)
        for copy in arrivals(i):
            copy.wait()
        base[:, at_] = base[:, at_] - dot3((vh[...], vl[...]), (zh[at_], zl[at_]), NT)
        leaving(i).start()

    for i in range(8):
        leaving(i).wait()


def local(matrix, reflectors, factor):
    vmem = pltpu.VMEM
    dma = pltpu.SemaphoreType.DMA
    nq = CHUNKS
    kc = 512 // nq
    sums = []
    for width in (256, 128):
        for rows in ((512,), (256,), (256,), (7, 32), (32,), (3, 8), (8,), (3, 8), (512,)):
            sums.append(vmem((*rows, width), F32))
    sems = []
    for groups in [7] * (2 * nq) + [2] * (2 * nq) + [1] * 14:
        sems += [dma((1,)), dma((groups,))]
    block, panel, tall, wide = (512, 2048), (512, 512), (nq, 2048, kc), (nq, 512, kc)
    piece, flat = (nq, 64, kc), (2048, 512)
    base, z_high, z_low = pl.pallas_call(
        kernel,
        out_shape=[
            jax.ShapeDtypeStruct(block, F32), jax.ShapeDtypeStruct(flat, BF16), jax.ShapeDtypeStruct(flat, BF16)
        ],
        in_specs=[pl.BlockSpec(memory_space=pl.ANY)] * 3,
        out_specs=[pl.BlockSpec(memory_space=pl.ANY)] * 3,
        scratch_shapes=[
            vmem(block, F32), vmem(block, F32), vmem(panel, F32), vmem(panel, F32), vmem(block, BF16), vmem(block, BF16),
            vmem(panel, BF16), vmem(panel, BF16), vmem(panel, BF16), vmem(panel, BF16),
            vmem(tall, F32), vmem(flat, BF16), vmem(flat, BF16), vmem(tall, F32), vmem(flat, BF16), vmem(flat, BF16),
            vmem(panel, BF16), vmem(panel, BF16), vmem(wide, F32), vmem((nq, 3, 2, 64, kc), F32),
            vmem(piece, F32), vmem(piece, F32), vmem(piece, F32), vmem(piece, BF16), vmem(piece, BF16), vmem(piece, F32),
            vmem(wide, F32), vmem(panel, BF16), vmem(panel, BF16),
            vmem(panel, BF16), vmem(panel, BF16), dma((3,)), dma((8 + 2 * nq,)), *sums, *sems,
        ],
        compiler_params=pltpu.CompilerParams(collective_id=0, has_side_effects=True, vmem_limit_bytes=56 << 20),
        name="panel_update",
    )(matrix, reflectors, factor)
    return pl.pallas_call(
        last_kernel,
        out_shape=jax.ShapeDtypeStruct(block, F32),
        in_specs=[pl.BlockSpec(memory_space=pl.ANY)] * 4,
        out_specs=pl.BlockSpec(memory_space=pl.ANY),
        scratch_shapes=[
            vmem(panel, F32), vmem(block, F32), vmem(flat, BF16), vmem(flat, BF16), vmem(panel, BF16), vmem(panel, BF16),
            dma((3, 8)), dma((9,)),
        ],
        compiler_params=pltpu.CompilerParams(vmem_limit_bytes=60 << 20),
        name="last_product",
    )(reflectors, base, z_high, z_low)


def solution(mesh):
    placed = (P("row", "col"), P("row", None), P())
    return jax.shard_map(
        local, mesh=mesh, in_specs=placed, out_specs=P("row", "col"), check_vma=False
    )
```
